256 devices in a mesh: depth: 64 (over x_lo, z, y), lat: 4 (over x_hi, core).
Axes of the slice: x: 4 (x_hi: 2, x_lo: 2; x = x_hi * 2 + x_lo), y: 4, z: 8, core: 2. Of those that a mesh axis runs over, the one named last changes fastest.
Arguments:
- incident: float32 [64, 2, 2, 128, 128], P('depth', None, None, 'lat'), may hold values from -6 to 6
- contrast: float32 [64, 128, 128], P('depth', 'lat'), may hold values from -0.8 to 0.8
- kernel: bfloat16 [64, 64, 2, 256, 256], P('depth', None, None, 'lat'), may hold values from -6 to 6
Outputs:
- total_field: float32 [64, 2, 2, 128, 128], P('depth', None, None, 'lat')
The draws below stay inside these ranges and needn't reach their ends.
All inputs are finite; a program needn't handle non-finite values.
Results may differ from the reference program's by a relative error of at most 0.017.
Values may be sent and summed in bfloat16 or wider, within the bound.
No kernel may reach another device: no remote copies, remote signals or barrier semaphores. Data moves between devices by JAX's collectives and lax.ppermute only.
A program may use at most 64 MiB of HBM per device.

```python
import math
import jax
import jax.numpy as jnp
from jax import lax

L = 128
SRC = 2
ITERS = 3
NZ = 64
P_SIZE = 256


def shard_levels(own_key, shape, pieces, least, top_value):
    def one(position, blocks):
        steps = jax.random.uniform(jax.random.fold_in(jax.random.fold_in(own_key, 6), position), (blocks,), jnp.float32, least / len(pieces), top_value / len(pieces))
        return jnp.repeat(jnp.exp(steps), shape[position] // blocks).reshape((-1,) + (1,) * (len(shape) - position - 1))

    factor_of = one(*pieces[0])
    for cut in pieces[1:]:
        factor_of = factor_of * one(*cut)
    return factor_of


def noise(own_key, dims, width, reach, pieces=(), held_as=jnp.bfloat16):
    array = width * jax.random.normal(own_key, dims, jnp.float32)
    if pieces:
        array = array * shard_levels(own_key, dims, pieces, -0.22, 0.18)
    return jnp.clip(array, -reach, reach).astype(held_as)


def setup_inputs(seed: int = 0) -> dict:
    streams_of = jax.random.split(jax.random.key(seed), 4)
    return {
        "incident": noise(streams_of[0], (NZ, SRC, 2, L, L), 1.0, 6.0, ((0, 64), (3, 4)), jnp.float32),
        "contrast": jnp.clip(jax.random.uniform(streams_of[1], (NZ, L, L), jnp.float32, -0.8, 0.8) * shard_levels(streams_of[1], (NZ, L, L), ((0, 64), (1, 4)), -0.4, 0.0), -0.8, 0.8),
        "kernel": noise(streams_of[2], (NZ, NZ, 2, P_SIZE, P_SIZE), (3.0 / NZ ** 0.5), 6.0, ((0, 64), (3, 4))),
    }


def wave_tables(count_in, count_out, period):
    indices = (jnp.arange(count_in, dtype=jnp.int32)[:, None] * jnp.arange(count_out, dtype=jnp.int32)[None, :]) % period
    angles = indices.astype(jnp.float32) * (2.0 * math.pi / period)
    return jnp.cos(angles).astype(jnp.bfloat16), jnp.sin(angles).astype(jnp.bfloat16)


def as_float(values):
    return values.astype(jnp.float32)


def last_dot(left, right):
    return jnp.einsum("...a,ab->...b", as_float(left), as_float(right), precision=lax.Precision.HIGHEST)


def middle_dot(left, right):
    return jnp.einsum("...ak,ab->...kb", as_float(left), as_float(right), precision=lax.Precision.HIGHEST)


def forward_pass(values, cosine, sine_table, product):
    real_part = values[..., 0, :, :]
    imag_part = values[..., 1, :, :]
    out_real = product(real_part, cosine) + product(imag_part, sine_table)
    out_imag = product(imag_part, cosine) - product(real_part, sine_table)
    return jnp.stack([out_real, out_imag], axis=-3)


def inverse_pass(values, cosine, sine_table, product):
    real_part = values[..., 0, :, :]
    imag_part = values[..., 1, :, :]
    out_real = product(real_part, cosine) - product(imag_part, sine_table)
    out_imag = product(real_part, sine_table) + product(imag_part, cosine)
    return jnp.stack([out_real, out_imag], axis=-3)


def couple(kern_rows, spectra):
    kern_real = kern_rows[:, :, 0]
    kern_imag = kern_rows[:, :, 1]
    spec_real = spectra[:, :, 0]
    spec_imag = spectra[:, :, 1]
    form = "lwkm,wskm->lskm"
    high = lax.Precision.HIGHEST
    out_real = jnp.einsum(form, kern_real, spec_real, precision=high) - jnp.einsum(form, kern_imag, spec_imag, precision=high)
    out_imag = jnp.einsum(form, kern_real, spec_imag, precision=high) + jnp.einsum(form, kern_imag, spec_real, precision=high)
    return jnp.stack([out_real, out_imag], axis=2)


def reference(incident, contrast, kernel):
    period = 2 * L
    forward_cos, forward_sin = wave_tables(L, period, period)
    inverse_cos, inverse_sin = wave_tables(period, L, period)
    fields = incident
    for iteration in range(ITERS):
        sources = (contrast[:, None, None] * fields).astype(jnp.bfloat16)
        along_y = forward_pass(sources, forward_cos, forward_sin, last_dot).astype(jnp.bfloat16)
        spectra = as_float(forward_pass(along_y, forward_cos, forward_sin, middle_dot).astype(jnp.bfloat16))

        def one_row(kern_row):
            return couple(as_float(kern_row)[None], spectra)[0]

        scattered = lax.map(one_row, kernel).astype(jnp.bfloat16)
        along_x = inverse_pass(scattered, inverse_cos, inverse_sin, last_dot).astype(jnp.bfloat16)
        fields = incident + inverse_pass(along_x, inverse_cos, inverse_sin, middle_dot) / float(period * period)
    return fields
```

```python
import functools
import itertools
import math

import jax
import jax.numpy as jnp
import ml_dtypes
import numpy as np
from jax import lax
from jax.experimental import pallas as pl
from jax.experimental.pallas import tpu as pltpu
from jax.sharding import Mesh, PartitionSpec as P

L = 128
P_SIZE = 256
NZ = 64
SRC = 2
ITERS = 3
LATS = 4
SHARES = 8
KYS = P_SIZE // (LATS * SHARES)
XS = L // LATS
LANES = SRC * 2 * XS
SPEC = SRC * 2 * P_SIZE

NAMES = ("xl", "zh", "zl", "yh", "yl", "xh", "c")
SIZES = (2, 4, 2, 2, 2, 2, 2)
DEPTH = ("xl", "zh", "zl", "yh", "yl")
LAT = ("xh", "c")
SHARE = ("xl", "zl", "yl")


def bf16(array):
    return np.asarray(array, np.float32).astype(ml_dtypes.bfloat16)


def wave_tables(count_in, count_out):
    index = np.arange(count_in)[:, None] * np.arange(count_out)[None, :] % P_SIZE
    angles = index * (2.0 * math.pi / P_SIZE)
    return np.cos(angles), np.sin(angles)


def tables():
    cosine, sine = wave_tables(L, P_SIZE)
    fwd_y = np.concatenate([cosine.T, sine.T], axis=1)
    fwd_x = np.zeros((LATS, SRC, 2, XS, SRC, 2, P_SIZE))
    cos_x = cosine.reshape(LATS, XS, P_SIZE)
    sin_x = sine.reshape(LATS, XS, P_SIZE)
    for s in range(SRC):
        fwd_x[:, s, 0, :, s, 0] = cos_x
        fwd_x[:, s, 1, :, s, 0] = sin_x
        fwd_x[:, s, 0, :, s, 1] = -sin_x
        fwd_x[:, s, 1, :, s, 1] = cos_x
    inv_cos, inv_sin = wave_tables(P_SIZE, L)
    inv_x = np.zeros((SRC, 2, P_SIZE, LATS, SRC, 2, XS))
    icos_x = inv_cos.reshape(P_SIZE, LATS, XS)
    isin_x = inv_sin.reshape(P_SIZE, LATS, XS)
    for s in range(SRC):
        inv_x[s, 0, :, :, s, 0] = icos_x
        inv_x[s, 1, :, :, s, 0] = -isin_x
        inv_x[s, 0, :, :, s, 1] = isin_x
        inv_x[s, 1, :, :, s, 1] = icos_x
    inv_y = np.concatenate([inv_cos, inv_sin], axis=1)
    return (
        bf16(fwd_y),
        bf16(fwd_x.reshape(LATS * LANES, SPEC)),
        bf16(inv_x.reshape(SPEC, LATS * LANES)),
        bf16(inv_y),
    )


def send_sources(field_parts, contrast_ref, table_ref, out_ref):
    left, right = [], []
    for real_part, imag_part in field_parts:
        real_src = contrast_ref[...] * real_part
        imag_src = contrast_ref[...] * imag_part
        left += [real_src, imag_src]
        right += [imag_src, -real_src]
    both = jnp.concatenate(
        [jnp.concatenate(left, axis=0), jnp.concatenate(right, axis=0)], axis=1
    ).astype(jnp.bfloat16)
    along_y = lax.dot_general(
        table_ref[...], both, (((1,), (1,)), ((), ())), preferred_element_type=jnp.float32
    ).astype(jnp.bfloat16)
    pair = 2 * KYS
    for lat, xl, zh, zl, yh in itertools.product(
        range(LATS), range(2), range(4), range(2), range(2)
    ):
        src = ((lat * 2 + xl) * 2 + zl) * pair
        dst = ((((lat * 2 + xl) * 4 + zh) * 2 + zl) * 2 + yh) * pair
        out_ref[dst : dst + pair, :] = along_y[src : src + pair, :]


def first_body(incident_ref, contrast_ref, table_ref, out_ref):
    parts = [(incident_ref[s, 0], incident_ref[s, 1]) for s in range(SRC)]
    send_sources(parts, contrast_ref, table_ref, out_ref)


def field_of(recv_ref, incident_ref, inv_ref):
    waves = lax.dot_general(
        recv_ref[...], inv_ref[...], (((0,), (0,)), ((), ())),
        preferred_element_type=jnp.float32,
    )
    scale = 1.0 / float(P_SIZE * P_SIZE)
    parts = []
    for s in range(SRC):
        real_rows = waves[2 * s * XS : (2 * s + 1) * XS]
        imag_rows = waves[(2 * s + 1) * XS : (2 * s + 2) * XS]
        parts.append(
            (
                incident_ref[s, 0] + (real_rows[:, :L] - imag_rows[:, L:]) * scale,
                incident_ref[s, 1] + (real_rows[:, L:] + imag_rows[:, :L]) * scale,
            )
        )
    return parts


def next_body(recv_ref, incident_ref, contrast_ref, inv_ref, table_ref, out_ref):
    send_sources(field_of(recv_ref, incident_ref, inv_ref), contrast_ref, table_ref, out_ref)


def last_body(recv_ref, incident_ref, inv_ref, out_ref):
    for s, parts in enumerate(field_of(recv_ref, incident_ref, inv_ref)):
        for part in range(2):
            out_ref[s, part] = parts[part]


BLOCK = 4


def couple_body(me_ref, recv_ref, fwd_ref, inv_ref, *refs):
    kern_refs, out_ref, spec_ref, sum_ref = refs[:SHARES], *refs[SHARES:]
    rows = NZ * KYS
    half = 2 * LANES
    chunk = 128
    for start in range(0, rows, chunk):
        total = None
        for pair in range(LATS // 2):
            left = jnp.concatenate(
                [
                    recv_ref[(2 * pair + i) * rows + start : (2 * pair + i) * rows + start + chunk, :]
                    for i in range(2)
                ],
                axis=1,
            )
            part = jnp.dot(
                left,
                fwd_ref[pair * half : (pair + 1) * half, :],
                preferred_element_type=jnp.float32,
            )
            total = part if total is None else total + part
        spec_ref[start : start + chunk, :] = total.astype(jnp.bfloat16).astype(jnp.float32)

    for first in range(0, SHARES, BLOCK):

        def step(w, sums):
            spec = spec_ref[pl.ds(pl.multiple_of(w * KYS, KYS), KYS), :]
            out = []
            for j in range(BLOCK):
                kern = kern_refs[first + j][w].astype(jnp.float32)
                kern_real, kern_imag = kern[:KYS], kern[KYS:]
                for s in range(SRC):
                    at = 2 * s * P_SIZE
                    spec_real = spec[:, at : at + P_SIZE]
                    spec_imag = spec[:, at + P_SIZE : at + 2 * P_SIZE]
                    real_sum, imag_sum = sums[2 * (j * SRC + s)], sums[2 * (j * SRC + s) + 1]
                    out.append(real_sum + kern_real * spec_real - kern_imag * spec_imag)
                    out.append(imag_sum + kern_real * spec_imag + kern_imag * spec_real)
            return tuple(out)

        zero = jnp.zeros((KYS, P_SIZE), jnp.float32)
        sums = lax.fori_loop(0, NZ, step, (zero,) * (BLOCK * SRC * 2), unroll=2)
        for j in range(BLOCK):
            row = pl.multiple_of((me_ref[0] ^ (first + j)) * KYS, KYS)
            for n in range(2 * SRC):
                sum_ref[pl.ds(row, KYS), n * P_SIZE : (n + 1) * P_SIZE] = sums[
                    j * 2 * SRC + n
                ]

    along_x = jnp.dot(
        sum_ref[...].astype(jnp.bfloat16), inv_ref[...], preferred_element_type=jnp.float32
    ).astype(jnp.bfloat16)
    held = SHARES * KYS
    for lat in range(LATS):
        out_ref[lat * held : (lat + 1) * held, :] = along_x[:, lat * LANES : (lat + 1) * LANES]


VMEM = pl.BlockSpec(memory_space=pltpu.VMEM)
SMEM = pl.BlockSpec(memory_space=pltpu.SMEM)
ALL_ROWS = LATS * NZ * KYS


def call(body, out, args, specs=None, scratch=(), flops=0):
    size = sum(math.prod(a.shape) * a.dtype.itemsize for a in args)
    return pl.pallas_call(
        body,
        out_shape=out,
        in_specs=specs or [VMEM] * len(args),
        out_specs=VMEM,
        scratch_shapes=list(scratch),
        compiler_params=pltpu.CompilerParams(vmem_limit_bytes=24 * 1024 * 1024),
        cost_estimate=pl.CostEstimate(flops=flops, bytes_accessed=size, transcendentals=0),
    )(*args)


def swap_perm(offset):
    pairs = []
    for place in range(SHARES):
        pairs.append((place, place ^ offset))
    return pairs


def local(incident, contrast, kernel):
    fwd_y, fwd_x, inv_x, inv_y = (jnp.asarray(t) for t in tables())
    incident = incident[0]
    contrast = contrast[0]
    me = lax.axis_index(SHARE).astype(jnp.int32)
    kern = kernel[0].reshape(NZ, 2, SHARES, KYS, P_SIZE)

    with jax.named_scope("kernel_exchange"):
        slabs = []
        for offset in range(SHARES):
            piece = lax.dynamic_index_in_dim(kern, me ^ offset, axis=2, keepdims=False)
            piece = piece.reshape(NZ, 2 * KYS, P_SIZE)
            if offset:
                piece = lax.ppermute(piece, SHARE, swap_perm(offset))
            slabs.append(piece)

    send_shape = jax.ShapeDtypeStruct((ALL_ROWS, LANES), jnp.bfloat16)
    back_shape = jax.ShapeDtypeStruct((LATS * SHARES * KYS, LANES), jnp.bfloat16)
    field_shape = jax.ShapeDtypeStruct((SRC, 2, XS, L), jnp.float32)
    sent = call(first_body, send_shape, (incident, contrast, fwd_y), flops=10**7)
    for iteration in range(ITERS):
        with jax.named_scope("to_wavenumbers"):
            got = lax.all_to_all(sent, LAT + DEPTH, 0, 0, tiled=True)
        back = call(
            couple_body,
            back_shape,
            (me.reshape(1), got, fwd_x, inv_x, *slabs),
            specs=[SMEM] + [VMEM] * (3 + SHARES),
            scratch=[
                pltpu.VMEM((NZ * KYS, SPEC), jnp.float32),
                pltpu.VMEM((SHARES * KYS, SPEC), jnp.float32),
            ],
            flops=10**9,
        )
        with jax.named_scope("to_rows"):
            rows = lax.all_to_all(back, LAT + SHARE, 0, 0, tiled=True)
        if iteration < ITERS - 1:
            sent = call(
                next_body, send_shape, (rows, incident, contrast, inv_y, fwd_y), flops=10**7
            )
    fields = call(last_body, field_shape, (rows, incident, inv_y), flops=10**7)
    return fields[None]


def solution(mesh):
    fine = Mesh(mesh.devices.reshape(SIZES), NAMES)
    in_specs = (
        P(DEPTH, None, None, LAT, None),
        P(DEPTH, LAT, None),
        P(DEPTH, None, None, LAT, None),
    )
    out_specs = P(DEPTH, None, None, LAT, None)
    return jax.shard_map(local, mesh=fine, in_specs=in_specs, out_specs=out_specs, check_vma=False)
```

```python
import itertools
import math

import jax
import jax.numpy as jnp
import ml_dtypes
import numpy as np
from jax import lax
from jax.experimental import pallas as pl
from jax.experimental.pallas import tpu as pltpu
from jax.sharding import Mesh, PartitionSpec as P

L = 128
P_SIZE = 256
NZ = 64
SRC = 2
ITERS = 3
LATS = 4
SHARES = 8
KYS = P_SIZE // (LATS * SHARES)
XS = L // LATS
LANES = SRC * 2 * XS
SPEC = SRC * 2 * P_SIZE

NAMES = ("xl", "zh", "zl", "yh", "yl", "xh", "c")
SIZES = (2, 4, 2, 2, 2, 2, 2)
DEPTH = ("xl", "zh", "zl", "yh", "yl")
LAT = ("xh", "c")
SHARE = ("xl", "zl", "yl")


def bf16(array):
    return np.asarray(array, np.float32).astype(ml_dtypes.bfloat16)


def wave_tables(count_in, count_out):
    index = np.arange(count_in)[:, None] * np.arange(count_out)[None, :] % P_SIZE
    angles = index * (2.0 * math.pi / P_SIZE)
    return np.cos(angles), np.sin(angles)


def tables():
    cosine, sine = wave_tables(L, P_SIZE)
    fwd_y = np.concatenate([cosine.T, sine.T], axis=1)
    fwd_x = np.zeros((LATS, SRC, 2, XS, SRC, 2, P_SIZE))
    cos_x = cosine.reshape(LATS, XS, P_SIZE)
    sin_x = sine.reshape(LATS, XS, P_SIZE)
    for s in range(SRC):
        fwd_x[:, s, 0, :, s, 0] = cos_x
        fwd_x[:, s, 1, :, s, 0] = sin_x
        fwd_x[:, s, 0, :, s, 1] = -sin_x
        fwd_x[:, s, 1, :, s, 1] = cos_x
    inv_cos, inv_sin = wave_tables(P_SIZE, L)
    inv_x = np.zeros((SRC, 2, P_SIZE, LATS, SRC, 2, XS))
    icos_x = inv_cos.reshape(P_SIZE, LATS, XS)
    isin_x = inv_sin.reshape(P_SIZE, LATS, XS)
    for s in range(SRC):
        inv_x[s, 0, :, :, s, 0] = icos_x
        inv_x[s, 1, :, :, s, 0] = -isin_x
        inv_x[s, 0, :, :, s, 1] = isin_x
        inv_x[s, 1, :, :, s, 1] = icos_x
    inv_y = np.concatenate([inv_cos, inv_sin], axis=1)
    return (
        bf16(fwd_y),
        bf16(fwd_x.reshape(LATS * LANES, SPEC)),
        bf16(inv_x.reshape(SPEC, LATS * LANES)),
        bf16(inv_y),
    )


def send_sources(field_parts, contrast_ref, table_ref, out_ref):
    left, right = [], []
    for real_part, imag_part in field_parts:
        real_src = contrast_ref[...] * real_part
        imag_src = contrast_ref[...] * imag_part
        left += [real_src, imag_src]
        right += [imag_src, -real_src]
    both = jnp.concatenate(
        [jnp.concatenate(left, axis=0), jnp.concatenate(right, axis=0)], axis=1
    ).astype(jnp.bfloat16)
    along_y = lax.dot_general(
        table_ref[...], both, (((1,), (1,)), ((), ())), preferred_element_type=jnp.float32
    ).astype(jnp.bfloat16)
    pair = 2 * KYS
    for lat, xl, zh, zl, yh in itertools.product(
        range(LATS), range(2), range(4), range(2), range(2)
    ):
        src = ((lat * 2 + xl) * 2 + zl) * pair
        dst = ((((lat * 2 + xl) * 4 + zh) * 2 + zl) * 2 + yh) * pair
        out_ref[dst : dst + pair, :] = along_y[src : src + pair, :]


def first_body(incident_ref, contrast_ref, table_ref, out_ref):
    parts = [(incident_ref[s, 0], incident_ref[s, 1]) for s in range(SRC)]
    send_sources(parts, contrast_ref, table_ref, out_ref)


def field_of(recv_ref, incident_ref, inv_ref):
    waves = lax.dot_general(
        recv_ref[...], inv_ref[...], (((0,), (0,)), ((), ())),
        preferred_element_type=jnp.float32,
    )
    scale = 1.0 / float(P_SIZE * P_SIZE)
    parts = []
    for s in range(SRC):
        real_rows = waves[2 * s * XS : (2 * s + 1) * XS]
        imag_rows = waves[(2 * s + 1) * XS : (2 * s + 2) * XS]
        parts.append(
            (
                incident_ref[s, 0] + (real_rows[:, :L] - imag_rows[:, L:]) * scale,
                incident_ref[s, 1] + (real_rows[:, L:] + imag_rows[:, :L]) * scale,
            )
        )
    return parts


def next_body(recv_ref, incident_ref, contrast_ref, inv_ref, table_ref, out_ref):
    send_sources(field_of(recv_ref, incident_ref, inv_ref), contrast_ref, table_ref, out_ref)


def last_body(recv_ref, incident_ref, inv_ref, out_ref):
    for s, parts in enumerate(field_of(recv_ref, incident_ref, inv_ref)):
        for part in range(2):
            out_ref[s, part] = parts[part]


SENT = (1, 2, 3, 4, 5, 6, 7)
COUPLE_MIB = 52
BLOCK = 2


def load_slabs(slab_refs, kern_ref, arrived):
    copies = [
        pltpu.make_async_copy(slab, kern_ref.at[n], arrived.at[n])
        for n, slab in enumerate(slab_refs)
    ]
    for copy in copies:
        copy.start()
    return copies


def transform_x(recv_ref, fwd_ref, spec_ref):
    rows = NZ * KYS
    half = 2 * LANES
    chunk = 128
    for start in range(0, rows, chunk):
        total = None
        for pair in range(LATS // 2):
            at = 2 * pair * rows + start
            left = jnp.concatenate(
                [recv_ref[at : at + chunk, :], recv_ref[at + rows : at + rows + chunk, :]], axis=1
            )
            part = jnp.dot(
                left,
                fwd_ref[pair * half : (pair + 1) * half, :],
                preferred_element_type=jnp.float32,
            )
            total = part if total is None else total + part
        spec_ref[start : start + chunk, :] = total.astype(jnp.bfloat16).astype(jnp.float32)


def couple(spec_ref, kern_ref, copies, put):
    count = len(copies)
    for first in range(0, count, BLOCK):
        block = range(first, min(first + BLOCK, count))
        for n in block:
            copies[n].wait()

        def step(w, sums, block=block):
            spec = spec_ref[pl.ds(pl.multiple_of(w * KYS, KYS), KYS), :]
            out = []
            for j, n in enumerate(block):
                kern = kern_ref[n, w].astype(jnp.float32)
                kern_real, kern_imag = kern[:KYS], kern[KYS:]
                for s in range(SRC):
                    at = 2 * s * P_SIZE
                    spec_real = spec[:, at : at + P_SIZE]
                    spec_imag = spec[:, at + P_SIZE : at + 2 * P_SIZE]
                    real_sum, imag_sum = sums[2 * (j * SRC + s)], sums[2 * (j * SRC + s) + 1]
                    out.append(real_sum + kern_real * spec_real - kern_imag * spec_imag)
                    out.append(imag_sum + kern_real * spec_imag + kern_imag * spec_real)
            return tuple(out)

        zero = jnp.zeros((KYS, P_SIZE), jnp.float32)
        sums = lax.fori_loop(0, NZ, step, (zero,) * (len(block) * SRC * 2), unroll=4)
        for j, n in enumerate(block):
            for quarter in range(2 * SRC):
                put(n, quarter, sums[j * 2 * SRC + quarter])


def put_by_place(me_ref, offsets, sum_ref):
    def put(n, quarter, total):
        row = pl.multiple_of((me_ref[0] ^ offsets[n]) * KYS, KYS)
        sum_ref[pl.ds(row, KYS), quarter * P_SIZE : (quarter + 1) * P_SIZE] = total

    return put


def invert_x(sum_ref, inv_ref, out_ref):
    along_x = jnp.dot(
        sum_ref[...].astype(jnp.bfloat16), inv_ref[...], preferred_element_type=jnp.float32
    ).astype(jnp.bfloat16)
    held = SHARES * KYS
    for lat in range(LATS):
        out_ref[lat * held : (lat + 1) * held, :] = along_x[:, lat * LANES : (lat + 1) * LANES]


def couple_body(me_ref, recv_hbm, fwd_ref, inv_ref, *refs):
    slab_refs, refs = refs[:SHARES], refs[SHARES:]
    out_ref, spec_ref, sum_ref, recv_ref, loaded, kern_ref, arrived = refs
    recv_copy = pltpu.make_async_copy(recv_hbm, recv_ref, loaded)
    recv_copy.start()
    slab_copies = load_slabs(slab_refs, kern_ref, arrived)
    recv_copy.wait()
    transform_x(recv_ref, fwd_ref, spec_ref)
    couple(spec_ref, kern_ref, slab_copies, put_by_place(me_ref, range(SHARES), sum_ref))
    invert_x(sum_ref, inv_ref, out_ref)


VMEM = pl.BlockSpec(memory_space=pltpu.VMEM)
SMEM = pl.BlockSpec(memory_space=pltpu.SMEM)
HBM = pl.BlockSpec(memory_space=pltpu.HBM)
ALL_ROWS = LATS * NZ * KYS


def call(body, out, args, specs=None, scratch=(), flops=0, mib=24):
    size = sum(math.prod(a.shape) * a.dtype.itemsize for a in args)
    return pl.pallas_call(
        body,
        out_shape=out,
        in_specs=specs or [VMEM] * len(args),
        out_specs=jax.tree.map(lambda _: VMEM, out),
        scratch_shapes=list(scratch),
        compiler_params=pltpu.CompilerParams(vmem_limit_bytes=mib * 1024 * 1024),
        cost_estimate=pl.CostEstimate(flops=flops, bytes_accessed=size, transcendentals=0),
    )(*args)


def swap_perm(offset):
    pairs = []
    for place in range(SHARES):
        pairs.append((place, place ^ offset))
    return pairs


def local(incident, contrast, kernel):
    fwd_y, fwd_x, inv_x, inv_y = (jnp.asarray(t) for t in tables())
    incident = incident[0]
    contrast = contrast[0]
    me = lax.axis_index(SHARE).astype(jnp.int32)
    me = me.reshape(1)
    kern = kernel[0].reshape(NZ, 2, SHARES, KYS, P_SIZE)

    with jax.named_scope("kernel_exchange"):
        slabs = [None] * SHARES
        for offset in (0,) + SENT:
            piece = lax.dynamic_index_in_dim(kern, me[0] ^ offset, axis=2, keepdims=False)
            piece = piece.reshape(NZ, 2 * KYS, P_SIZE)
            slabs[offset] = lax.ppermute(piece, SHARE, swap_perm(offset)) if offset else piece

    send_shape = jax.ShapeDtypeStruct((ALL_ROWS, LANES), jnp.bfloat16)
    back_shape = jax.ShapeDtypeStruct((LATS * SHARES * KYS, LANES), jnp.bfloat16)
    field_shape = jax.ShapeDtypeStruct((SRC, 2, XS, L), jnp.float32)
    sent = call(first_body, send_shape, (incident, contrast, fwd_y), flops=10**7)
    for iteration in range(ITERS):
        with jax.named_scope("to_wavenumbers"):
            got = lax.all_to_all(sent, LAT + DEPTH, 0, 0, tiled=True)
        back = call(
            couple_body,
            back_shape,
            (me, got, fwd_x, inv_x, *slabs),
            specs=[SMEM, HBM, VMEM, VMEM] + [HBM] * SHARES,
            scratch=[
                pltpu.VMEM((NZ * KYS, SPEC), jnp.float32),
                pltpu.VMEM((SHARES * KYS, SPEC), jnp.float32),
                pltpu.VMEM((ALL_ROWS, LANES), jnp.bfloat16),
                pltpu.SemaphoreType.DMA,
                pltpu.VMEM((SHARES, NZ, 2 * KYS, P_SIZE), jnp.bfloat16),
                pltpu.SemaphoreType.DMA((SHARES,)),
            ],
            flops=10**9,
            mib=COUPLE_MIB,
        )
        with jax.named_scope("to_rows"):
            rows = lax.all_to_all(back, LAT + SHARE, 0, 0, tiled=True)
        if iteration < ITERS - 1:
            sent = call(
                next_body, send_shape, (rows, incident, contrast, inv_y, fwd_y), flops=10**7
            )
    fields = call(last_body, field_shape, (rows, incident, inv_y), flops=10**7)
    return fields[None]


def solution(mesh):
    fine = Mesh(mesh.devices.reshape(SIZES), NAMES)
    in_specs = (
        P(DEPTH, None, None, LAT, None),
        P(DEPTH, LAT, None),
        P(DEPTH, None, None, LAT, None),
    )
    out_specs = P(DEPTH, None, None, LAT, None)
    return jax.shard_map(local, mesh=fine, in_specs=in_specs, out_specs=out_specs, check_vma=False)
```

```python
import itertools
import math

import jax
import jax.numpy as jnp
import ml_dtypes
import numpy as np
from jax import lax
from jax.experimental import pallas as pl
from jax.experimental.pallas import tpu as pltpu
from jax.sharding import Mesh, PartitionSpec as P

L = 128
P_SIZE = 256
NZ = 64
SRC = 2
ITERS = 3
LATS = 4
SHARES = 8
KYS = P_SIZE // (LATS * SHARES)
XS = L // LATS
LANES = SRC * 2 * XS
SPEC = SRC * 2 * P_SIZE

NAMES = ("xl", "zh", "zl", "yh", "yl", "xh", "c")
SIZES = (2, 4, 2, 2, 2, 2, 2)
DEPTH = ("xl", "zh", "zl", "yh", "yl")
LAT = ("xh", "c")
SHARE = ("xl", "zl", "yl")


def bf16(array):
    return np.asarray(array, np.float32).astype(ml_dtypes.bfloat16)


def wave_tables(count_in, count_out):
    index = np.arange(count_in)[:, None] * np.arange(count_out)[None, :] % P_SIZE
    angles = index * (2.0 * math.pi / P_SIZE)
    return np.cos(angles), np.sin(angles)


def tables():
    cosine, sine = wave_tables(L, P_SIZE)
    fwd_y = np.concatenate([cosine.T, sine.T], axis=1)
    fwd_x = np.zeros((LATS, SRC, 2, XS, SRC, 2, P_SIZE))
    cos_x = cosine.reshape(LATS, XS, P_SIZE)
    sin_x = sine.reshape(LATS, XS, P_SIZE)
    for s in range(SRC):
        fwd_x[:, s, 0, :, s, 0] = cos_x
        fwd_x[:, s, 1, :, s, 0] = sin_x
        fwd_x[:, s, 0, :, s, 1] = -sin_x
        fwd_x[:, s, 1, :, s, 1] = cos_x
    inv_cos, inv_sin = wave_tables(P_SIZE, L)
    inv_x = np.zeros((SRC, 2, P_SIZE, LATS, SRC, 2, XS))
    icos_x = inv_cos.reshape(P_SIZE, LATS, XS)
    isin_x = inv_sin.reshape(P_SIZE, LATS, XS)
    for s in range(SRC):
        inv_x[s, 0, :, :, s, 0] = icos_x
        inv_x[s, 1, :, :, s, 0] = -isin_x
        inv_x[s, 0, :, :, s, 1] = isin_x
        inv_x[s, 1, :, :, s, 1] = icos_x
    inv_y = np.concatenate([inv_cos, inv_sin], axis=1)
    return (
        bf16(fwd_y),
        bf16(fwd_x.reshape(LATS * LANES, SPEC)),
        bf16(inv_x.reshape(SPEC, LATS * LANES)),
        bf16(inv_y),
    )


def send_sources(field_parts, contrast_ref, table_ref, out_ref):
    left, right = [], []
    for real_part, imag_part in field_parts:
        real_src = contrast_ref[...] * real_part
        imag_src = contrast_ref[...] * imag_part
        left += [real_src, imag_src]
        right += [imag_src, -real_src]
    both = jnp.concatenate(
        [jnp.concatenate(left, axis=0), jnp.concatenate(right, axis=0)], axis=1
    ).astype(jnp.bfloat16)
    along_y = lax.dot_general(
        table_ref[...], both, (((1,), (1,)), ((), ())), preferred_element_type=jnp.float32
    ).astype(jnp.bfloat16)
    pair = 2 * KYS
    for lat, xl, zh, zl, yh in itertools.product(
        range(LATS), range(2), range(4), range(2), range(2)
    ):
        src = ((lat * 2 + xl) * 2 + zl) * pair
        dst = ((((lat * 2 + xl) * 4 + zh) * 2 + zl) * 2 + yh) * pair
        out_ref[dst : dst + pair, :] = along_y[src : src + pair, :]


def first_body(incident_ref, contrast_ref, table_ref, out_ref):
    parts = [(incident_ref[s, 0], incident_ref[s, 1]) for s in range(SRC)]
    send_sources(parts, contrast_ref, table_ref, out_ref)


def field_of(recv_ref, incident_ref, inv_ref):
    waves = lax.dot_general(
        recv_ref[...], inv_ref[...], (((0,), (0,)), ((), ())),
        preferred_element_type=jnp.float32,
    )
    scale = 1.0 / float(P_SIZE * P_SIZE)
    parts = []
    for s in range(SRC):
        real_rows = waves[2 * s * XS : (2 * s + 1) * XS]
        imag_rows = waves[(2 * s + 1) * XS : (2 * s + 2) * XS]
        parts.append(
            (
                incident_ref[s, 0] + (real_rows[:, :L] - imag_rows[:, L:]) * scale,
                incident_ref[s, 1] + (real_rows[:, L:] + imag_rows[:, :L]) * scale,
            )
        )
    return parts


def next_body(recv_ref, incident_ref, contrast_ref, inv_ref, table_ref, out_ref):
    send_sources(field_of(recv_ref, incident_ref, inv_ref), contrast_ref, table_ref, out_ref)


def last_body(recv_ref, incident_ref, inv_ref, out_ref):
    for s, parts in enumerate(field_of(recv_ref, incident_ref, inv_ref)):
        for part in range(2):
            out_ref[s, part] = parts[part]


CUT_GROUPS = ((6, 7), (0, 1, 2, 3, 4, 5))
COUPLE_MIB = 52
BLOCK = 2


def load_slabs(slab_refs, kern_ref, arrived):
    copies = [
        pltpu.make_async_copy(slab, kern_ref.at[n], arrived.at[n])
        for n, slab in enumerate(slab_refs)
    ]
    for copy in copies:
        copy.start()
    return copies


def transform_x(recv_ref, fwd_ref, spec_ref):
    rows = NZ * KYS
    half = 2 * LANES
    chunk = 128
    for start in range(0, rows, chunk):
        total = None
        for pair in range(LATS // 2):
            at = 2 * pair * rows + start
            left = jnp.concatenate(
                [recv_ref[at : at + chunk, :], recv_ref[at + rows : at + rows + chunk, :]], axis=1
            )
            part = jnp.dot(
                left,
                fwd_ref[pair * half : (pair + 1) * half, :],
                preferred_element_type=jnp.float32,
            )
            total = part if total is None else total + part
        spec_ref[start : start + chunk, :] = total.astype(jnp.bfloat16).astype(jnp.float32)


def couple(spec_ref, kern_ref, copies, put):
    count = len(copies)
    for first in range(0, count, BLOCK):
        block = range(first, min(first + BLOCK, count))
        for n in block:
            copies[n].wait()

        def step(w, sums, block=block):
            spec = spec_ref[pl.ds(pl.multiple_of(w * KYS, KYS), KYS), :]
            out = []
            for j, n in enumerate(block):
                kern = kern_ref[n, w].astype(jnp.float32)
                kern_real, kern_imag = kern[:KYS], kern[KYS:]
                for s in range(SRC):
                    at = 2 * s * P_SIZE
                    spec_real = spec[:, at : at + P_SIZE]
                    spec_imag = spec[:, at + P_SIZE : at + 2 * P_SIZE]
                    real_sum, imag_sum = sums[2 * (j * SRC + s)], sums[2 * (j * SRC + s) + 1]
                    out.append(real_sum + kern_real * spec_real - kern_imag * spec_imag)
                    out.append(imag_sum + kern_real * spec_imag + kern_imag * spec_real)
            return tuple(out)

        zero = jnp.zeros((KYS, P_SIZE), jnp.float32)
        sums = lax.fori_loop(0, NZ, step, (zero,) * (len(block) * SRC * 2), unroll=8)
        for j, n in enumerate(block):
            for quarter in range(2 * SRC):
                put(n, quarter, sums[j * 2 * SRC + quarter])


def put_by_place(me_ref, offsets, sum_ref):
    def put(n, quarter, total):
        row = pl.multiple_of((me_ref[0] ^ offsets[n]) * KYS, KYS)
        sum_ref[pl.ds(row, KYS), quarter * P_SIZE : (quarter + 1) * P_SIZE] = total

    return put


def invert_x(sum_ref, inv_ref, out_ref):
    along_x = jnp.dot(
        sum_ref[...].astype(jnp.bfloat16), inv_ref[...], preferred_element_type=jnp.float32
    ).astype(jnp.bfloat16)
    held = SHARES * KYS
    for lat in range(LATS):
        out_ref[lat * held : (lat + 1) * held, :] = along_x[:, lat * LANES : (lat + 1) * LANES]


def couple_body(me_ref, recv_hbm, fwd_ref, inv_ref, *refs):
    slab_refs, refs = refs[:SHARES], refs[SHARES:]
    out_ref, spec_ref, sum_ref, recv_ref, loaded, kern_ref, arrived = refs
    recv_copy = pltpu.make_async_copy(recv_hbm, recv_ref, loaded)
    recv_copy.start()
    slab_copies = load_slabs(slab_refs, kern_ref, arrived)
    recv_copy.wait()
    transform_x(recv_ref, fwd_ref, spec_ref)
    couple(spec_ref, kern_ref, slab_copies, put_by_place(me_ref, range(SHARES), sum_ref))
    invert_x(sum_ref, inv_ref, out_ref)


VMEM = pl.BlockSpec(memory_space=pltpu.VMEM)
SMEM = pl.BlockSpec(memory_space=pltpu.SMEM)
HBM = pl.BlockSpec(memory_space=pltpu.HBM)
ALL_ROWS = LATS * NZ * KYS


def call(body, out, args, specs=None, scratch=(), flops=0, mib=24):
    size = sum(math.prod(a.shape) * a.dtype.itemsize for a in args)
    return pl.pallas_call(
        body,
        out_shape=out,
        in_specs=specs or [VMEM] * len(args),
        out_specs=jax.tree.map(lambda _: VMEM, out),
        scratch_shapes=list(scratch),
        compiler_params=pltpu.CompilerParams(vmem_limit_bytes=mib * 1024 * 1024),
        cost_estimate=pl.CostEstimate(flops=flops, bytes_accessed=size, transcendentals=0),
    )(*args)


def swap_perm(offset):
    pairs = []
    for place in range(SHARES):
        pairs.append((place, place ^ offset))
    return pairs


def local(incident, contrast, kernel):
    fwd_y, fwd_x, inv_x, inv_y = (jnp.asarray(t) for t in tables())
    incident = incident[0]
    contrast = contrast[0]
    me = lax.axis_index(SHARE).astype(jnp.int32)
    me = me.reshape(1)
    kern = kernel[0].reshape(NZ, 2, SHARES, KYS, P_SIZE)

    with jax.named_scope("kernel_exchange"):
        pieces = {}
        place = me[0]
        for group in CUT_GROUPS:
            for offset in group:
                piece = lax.dynamic_index_in_dim(kern, place ^ offset, axis=2, keepdims=False)
                pieces[offset] = piece.reshape(NZ, 2 * KYS, P_SIZE)
            first = group[0]
            pieces[first], place = lax.optimization_barrier((pieces[first], place))
        slabs = [pieces[0]]
        for offset in range(1, SHARES):
            slabs.append(lax.ppermute(pieces[offset], SHARE, swap_perm(offset)))

    send_shape = jax.ShapeDtypeStruct((ALL_ROWS, LANES), jnp.bfloat16)
    back_shape = jax.ShapeDtypeStruct((LATS * SHARES * KYS, LANES), jnp.bfloat16)
    field_shape = jax.ShapeDtypeStruct((SRC, 2, XS, L), jnp.float32)
    sent = call(first_body, send_shape, (incident, contrast, fwd_y), flops=10**7)
    for iteration in range(ITERS):
        with jax.named_scope("to_wavenumbers"):
            got = lax.all_to_all(sent, LAT + DEPTH, 0, 0, tiled=True)
        back = call(
            couple_body,
            back_shape,
            (me, got, fwd_x, inv_x, *slabs),
            specs=[SMEM, HBM, VMEM, VMEM] + [HBM] * SHARES,
            scratch=[
                pltpu.VMEM((NZ * KYS, SPEC), jnp.float32),
                pltpu.VMEM((SHARES * KYS, SPEC), jnp.float32),
                pltpu.VMEM((ALL_ROWS, LANES), jnp.bfloat16),
                pltpu.SemaphoreType.DMA,
                pltpu.VMEM((SHARES, NZ, 2 * KYS, P_SIZE), jnp.bfloat16),
                pltpu.SemaphoreType.DMA((SHARES,)),
            ],
            flops=10**9,
            mib=COUPLE_MIB,
        )
        with jax.named_scope("to_rows"):
            rows = lax.all_to_all(back, LAT + SHARE, 0, 0, tiled=True)
        if iteration < ITERS - 1:
            sent = call(
                next_body, send_shape, (rows, incident, contrast, inv_y, fwd_y), flops=10**7
            )
    fields = call(last_body, field_shape, (rows, incident, inv_y), flops=10**7)
    return fields[None]


def solution(mesh):
    fine = Mesh(mesh.devices.reshape(SIZES), NAMES)
    in_specs = (
        P(DEPTH, None, None, LAT, None),
        P(DEPTH, LAT, None),
        P(DEPTH, None, None, LAT, None),
    )
    out_specs = P(DEPTH, None, None, LAT, None)
    return jax.shard_map(local, mesh=fine, in_specs=in_specs, out_specs=out_specs, check_vma=False)
```

```python
import itertools
import math

import jax
import jax.numpy as jnp
import ml_dtypes
import numpy as np
from jax import lax
from jax.experimental import pallas as pl
from jax.experimental.pallas import tpu as pltpu
from jax.sharding import Mesh, PartitionSpec as P

L = 128
P_SIZE = 256
NZ = 64
SRC = 2
ITERS = 3
LATS = 4
SHARES = 8
KYS = P_SIZE // (LATS * SHARES)
XS = L // LATS
LANES = SRC * 2 * XS
SPEC = SRC * 2 * P_SIZE

NAMES = ("xl", "zh", "zl", "yh", "yl", "xh", "c")
SIZES = (2, 4, 2, 2, 2, 2, 2)
DEPTH = ("xl", "zh", "zl", "yh", "yl")
LAT = ("xh", "c")
SHARE = ("xl", "zl", "yl")


def bf16(array):
    return np.asarray(array, np.float32).astype(ml_dtypes.bfloat16)


def wave_tables(count_in, count_out):
    index = np.arange(count_in)[:, None] * np.arange(count_out)[None, :] % P_SIZE
    angles = index * (2.0 * math.pi / P_SIZE)
    return np.cos(angles), np.sin(angles)


def tables():
    cosine, sine = wave_tables(L, P_SIZE)
    fwd_y = np.concatenate([cosine.T, sine.T], axis=1)
    fwd_x = np.zeros((LATS, SRC, 2, XS, SRC, 2, P_SIZE))
    cos_x = cosine.reshape(LATS, XS, P_SIZE)
    sin_x = sine.reshape(LATS, XS, P_SIZE)
    for s in range(SRC):
        fwd_x[:, s, 0, :, s, 0] = cos_x
        fwd_x[:, s, 1, :, s, 0] = sin_x
        fwd_x[:, s, 0, :, s, 1] = -sin_x
        fwd_x[:, s, 1, :, s, 1] = cos_x
    inv_cos, inv_sin = wave_tables(P_SIZE, L)
    inv_x = np.zeros((SRC, 2, P_SIZE, LATS, SRC, 2, XS))
    icos_x = inv_cos.reshape(P_SIZE, LATS, XS)
    isin_x = inv_sin.reshape(P_SIZE, LATS, XS)
    for s in range(SRC):
        inv_x[s, 0, :, :, s, 0] = icos_x
        inv_x[s, 1, :, :, s, 0] = -isin_x
        inv_x[s, 0, :, :, s, 1] = isin_x
        inv_x[s, 1, :, :, s, 1] = icos_x
    inv_y = np.concatenate([inv_cos, inv_sin], axis=1)
    return (
        bf16(fwd_y),
        bf16(fwd_x.reshape(LATS * LANES, SPEC)),
        bf16(inv_x.reshape(SPEC, LATS * LANES)),
        bf16(inv_y),
    )


def send_sources(field_parts, contrast_ref, table_ref, out_ref):
    left, right = [], []
    for real_part, imag_part in field_parts:
        real_src = contrast_ref[...] * real_part
        imag_src = contrast_ref[...] * imag_part
        left += [real_src, imag_src]
        right += [imag_src, -real_src]
    both = jnp.concatenate(
        [jnp.concatenate(left, axis=0), jnp.concatenate(right, axis=0)], axis=1
    ).astype(jnp.bfloat16)
    along_y = lax.dot_general(
        table_ref[...], both, (((1,), (1,)), ((), ())), preferred_element_type=jnp.float32
    ).astype(jnp.bfloat16)
    pair = 2 * KYS
    for lat, xl, zh, zl, yh in itertools.product(
        range(LATS), range(2), range(4), range(2), range(2)
    ):
        src = ((lat * 2 + xl) * 2 + zl) * pair
        dst = ((((lat * 2 + xl) * 4 + zh) * 2 + zl) * 2 + yh) * pair
        out_ref[dst : dst + pair, :] = along_y[src : src + pair, :]


def first_body(incident_ref, contrast_ref, table_ref, cut_ref, out_ref):
    del cut_ref
    parts = [(incident_ref[s, 0], incident_ref[s, 1]) for s in range(SRC)]
    send_sources(parts, contrast_ref, table_ref, out_ref)


def field_of(recv_ref, incident_ref, inv_ref):
    waves = lax.dot_general(
        recv_ref[...], inv_ref[...], (((0,), (0,)), ((), ())),
        preferred_element_type=jnp.float32,
    )
    scale = 1.0 / float(P_SIZE * P_SIZE)
    parts = []
    for s in range(SRC):
        real_rows = waves[2 * s * XS : (2 * s + 1) * XS]
        imag_rows = waves[(2 * s + 1) * XS : (2 * s + 2) * XS]
        parts.append(
            (
                incident_ref[s, 0] + (real_rows[:, :L] - imag_rows[:, L:]) * scale,
                incident_ref[s, 1] + (real_rows[:, L:] + imag_rows[:, :L]) * scale,
            )
        )
    return parts


def next_body(recv_ref, incident_ref, contrast_ref, inv_ref, table_ref, out_ref):
    send_sources(field_of(recv_ref, incident_ref, inv_ref), contrast_ref, table_ref, out_ref)


def last_body(recv_ref, incident_ref, inv_ref, out_ref):
    for s, parts in enumerate(field_of(recv_ref, incident_ref, inv_ref)):
        for part in range(2):
            out_ref[s, part] = parts[part]


CUT_GROUPS = ((6,), (7,), (5, 4, 3, 2, 1, 0))
COUPLE_MIB = 52
BLOCK = 2


def load_slabs(slab_refs, kern_ref, arrived):
    copies = [
        pltpu.make_async_copy(slab, kern_ref.at[n], arrived.at[n])
        for n, slab in enumerate(slab_refs)
    ]
    for copy in copies:
        copy.start()
    return copies


def transform_x(recv_ref, fwd_ref, spec_ref):
    rows = NZ * KYS
    half = 2 * LANES
    chunk = 128
    for start in range(0, rows, chunk):
        total = None
        for pair in range(LATS // 2):
            at = 2 * pair * rows + start
            left = jnp.concatenate(
                [recv_ref[at : at + chunk, :], recv_ref[at + rows : at + rows + chunk, :]], axis=1
            )
            part = jnp.dot(
                left,
                fwd_ref[pair * half : (pair + 1) * half, :],
                preferred_element_type=jnp.float32,
            )
            total = part if total is None else total + part
        spec_ref[start : start + chunk, :] = total.astype(jnp.bfloat16).astype(jnp.float32)


def couple(spec_ref, kern_ref, copies, put):
    count = len(copies)
    for first in range(0, count, BLOCK):
        block = range(first, min(first + BLOCK, count))
        for n in block:
            copies[n].wait()

        def step(w, sums, block=block):
            spec = spec_ref[pl.ds(pl.multiple_of(w * KYS, KYS), KYS), :]
            out = []
            for j, n in enumerate(block):
                kern = kern_ref[n, w].astype(jnp.float32)
                kern_real, kern_imag = kern[:KYS], kern[KYS:]
                for s in range(SRC):
                    at = 2 * s * P_SIZE
                    spec_real = spec[:, at : at + P_SIZE]
                    spec_imag = spec[:, at + P_SIZE : at + 2 * P_SIZE]
                    real_sum, imag_sum = sums[2 * (j * SRC + s)], sums[2 * (j * SRC + s) + 1]
                    out.append(real_sum + kern_real * spec_real - kern_imag * spec_imag)
                    out.append(imag_sum + kern_real * spec_imag + kern_imag * spec_real)
            return tuple(out)

        zero = jnp.zeros((KYS, P_SIZE), jnp.float32)
        sums = lax.fori_loop(0, NZ, step, (zero,) * (len(block) * SRC * 2), unroll=8)
        for j, n in enumerate(block):
            for quarter in range(2 * SRC):
                put(n, quarter, sums[j * 2 * SRC + quarter])


def put_by_place(me_ref, offsets, sum_ref):
    def put(n, quarter, total):
        row = pl.multiple_of((me_ref[0] ^ offsets[n]) * KYS, KYS)
        sum_ref[pl.ds(row, KYS), quarter * P_SIZE : (quarter + 1) * P_SIZE] = total

    return put


def invert_x(sum_ref, inv_ref, out_ref):
    along_x = jnp.dot(
        sum_ref[...].astype(jnp.bfloat16), inv_ref[...], preferred_element_type=jnp.float32
    ).astype(jnp.bfloat16)
    held = SHARES * KYS
    for lat in range(LATS):
        out_ref[lat * held : (lat + 1) * held, :] = along_x[:, lat * LANES : (lat + 1) * LANES]


def couple_body(me_ref, recv_hbm, fwd_ref, inv_ref, *refs):
    slab_refs, refs = refs[:SHARES], refs[SHARES:]
    out_ref, spec_ref, sum_ref, recv_ref, loaded, kern_ref, arrived = refs
    recv_copy = pltpu.make_async_copy(recv_hbm, recv_ref, loaded)
    recv_copy.start()
    slab_copies = load_slabs(slab_refs, kern_ref, arrived)
    recv_copy.wait()
    transform_x(recv_ref, fwd_ref, spec_ref)
    couple(spec_ref, kern_ref, slab_copies, put_by_place(me_ref, range(SHARES), sum_ref))
    invert_x(sum_ref, inv_ref, out_ref)


VMEM = pl.BlockSpec(memory_space=pltpu.VMEM)
SMEM = pl.BlockSpec(memory_space=pltpu.SMEM)
HBM = pl.BlockSpec(memory_space=pltpu.HBM)
ALL_ROWS = LATS * NZ * KYS


def call(body, out, args, specs=None, scratch=(), flops=0, mib=24):
    size = sum(math.prod(a.shape) * a.dtype.itemsize for a in args)
    return pl.pallas_call(
        body,
        out_shape=out,
        in_specs=specs or [VMEM] * len(args),
        out_specs=jax.tree.map(lambda _: VMEM, out),
        scratch_shapes=list(scratch),
        compiler_params=pltpu.CompilerParams(vmem_limit_bytes=mib * 1024 * 1024),
        cost_estimate=pl.CostEstimate(flops=flops, bytes_accessed=size, transcendentals=0),
    )(*args)


def swap_perm(offset):
    pairs = []
    for place in range(SHARES):
        pairs.append((place, place ^ offset))
    return pairs


def local(incident, contrast, kernel):
    fwd_y, fwd_x, inv_x, inv_y = (jnp.asarray(t) for t in tables())
    incident = incident[0]
    contrast = contrast[0]
    me = lax.axis_index(SHARE).astype(jnp.int32)
    me = me.reshape(1)
    kern = kernel[0].reshape(NZ, 2, SHARES, KYS, P_SIZE)

    with jax.named_scope("kernel_exchange"):
        pieces = {}
        place = me[0]
        for group in CUT_GROUPS:
            for offset in group:
                piece = lax.dynamic_index_in_dim(kern, place ^ offset, axis=2, keepdims=False)
                pieces[offset] = piece.reshape(NZ, 2 * KYS, P_SIZE)
            cut, place = lax.optimization_barrier(([pieces[j] for j in group], place))
            pieces.update(zip(group, cut))
        slabs = [pieces[0]]
        for offset in range(1, SHARES):
            slabs.append(lax.ppermute(pieces[offset], SHARE, swap_perm(offset)))

    send_shape = jax.ShapeDtypeStruct((ALL_ROWS, LANES), jnp.bfloat16)
    back_shape = jax.ShapeDtypeStruct((LATS * SHARES * KYS, LANES), jnp.bfloat16)
    field_shape = jax.ShapeDtypeStruct((SRC, 2, XS, L), jnp.float32)
    sent = call(
        first_body,
        send_shape,
        (incident, contrast, fwd_y, slabs[0]),
        specs=[VMEM] * 3 + [HBM],
        flops=10**7,
    )
    for iteration in range(ITERS):
        with jax.named_scope("to_wavenumbers"):
            got = lax.all_to_all(sent, LAT + DEPTH, 0, 0, tiled=True)
        back = call(
            couple_body,
            back_shape,
            (me, got, fwd_x, inv_x, *slabs),
            specs=[SMEM, HBM, VMEM, VMEM] + [HBM] * SHARES,
            scratch=[
                pltpu.VMEM((NZ * KYS, SPEC), jnp.float32),
                pltpu.VMEM((SHARES * KYS, SPEC), jnp.float32),
                pltpu.VMEM((ALL_ROWS, LANES), jnp.bfloat16),
                pltpu.SemaphoreType.DMA,
                pltpu.VMEM((SHARES, NZ, 2 * KYS, P_SIZE), jnp.bfloat16),
                pltpu.SemaphoreType.DMA((SHARES,)),
            ],
            flops=10**9,
            mib=COUPLE_MIB,
        )
        with jax.named_scope("to_rows"):
            rows = lax.all_to_all(back, LAT + SHARE, 0, 0, tiled=True)
        if iteration < ITERS - 1:
            sent = call(
                next_body, send_shape, (rows, incident, contrast, inv_y, fwd_y), flops=10**7
            )
    fields = call(last_body, field_shape, (rows, incident, inv_y), flops=10**7)
    return fields[None]


def solution(mesh):
    fine = Mesh(mesh.devices.reshape(SIZES), NAMES)
    in_specs = (
        P(DEPTH, None, None, LAT, None),
        P(DEPTH, LAT, None),
        P(DEPTH, None, None, LAT, None),
    )
    out_specs = P(DEPTH, None, None, LAT, None)
    return jax.shard_map(local, mesh=fine, in_specs=in_specs, out_specs=out_specs, check_vma=False)
```
